128 devices in a mesh: row: 8 (over x, core), col: 16 (over z, y).
Axes of the slice: x: 4, y: 4, z: 4, core: 2. Of those that a mesh axis runs over, the one named last changes fastest.
Arguments:
- panel: float32 [32768, 256], P(('row', 'col')), as said below
- trailing: float32 [32768, 4096], P('row', 'col'), may hold values from -6 to 6
- factors: bfloat16 [16384, 256, 128], P(('row', 'col')), may hold values from -1.1953125 to 1.1953125
- owner: int32 [16384, 1], P(('row', 'col')), may hold values from 0 to 127; in each aligned block of 128 rows (0 to 127, 128 to 255, ...) at most 2 rows name the same one
- tile_slot: int32 [16384], P(('row', 'col')), may hold values from 0 to 15
- ranks: int32 [16384], P(('row', 'col')), may hold values from 32 to 64
Outputs:
- updated: float32 [32768, 4096], P('row', 'col')
- lower: float32 [32768, 256], P(('row', 'col'))
The draws below stay inside these ranges and needn't reach their ends.
Inputs may be any that keep to these rules, and one draw needn't show every extreme that they name: Within the rows of one device no owner is named more than 2 times, a bound that some block reaches. `panel`: rows 0 to 255 form a symmetric positive definite block.
All inputs are finite; a program needn't handle non-finite values.
Results may differ from the reference program's by a relative error of at most 0.0003.
Values may be sent and summed in bfloat16 or wider, within the bound.
No kernel may reach another device: no remote copies, remote signals or barrier semaphores. Data moves between devices by JAX's collectives and lax.ppermute only.
A program may use at most 192 MiB of HBM per device.

```python
import math
import jax
import jax.numpy as jnp
import numpy as np
from jax import lax

TB = 256
RK = 64
ITEMS_DEV = 128
CAP = 2
ITEMS = 16384
M = 32768
W = 4096
N_COL = 16
DEVICES = 128


def draw_panel(key, part):
    key = jax.random.fold_in(key, 7)
    first_key, second_key = jax.random.split(key)
    others = jax.random.normal(first_key, (M, TB), jnp.float32) * 0.25
    seeds = jax.random.normal(second_key, (TB, TB), jnp.float32)
    block = jnp.dot(seeds, seeds.T, precision=lax.Precision.HIGHEST) / TB
    block = 0.25 * (block + block.T) + 1.5 * jnp.eye(TB, dtype=jnp.float32)
    return others.at[:TB].set(block)


def plant(values, stream_key, least, top_value):
    longest = values.shape.index(max(values.shape))
    spots = []
    for shift in (0, 1):
        where = [jax.random.randint(jax.random.fold_in(stream_key, axis), (), 0, length) for axis, length in enumerate(values.shape)]
        where[longest] = (where[longest] + shift) % values.shape[longest]
        spots.append(tuple(where))
    return values.at[spots[0]].set(least).at[spots[1]].set(top_value)


def level_of(own_key, dims, cuts, least, largest):
    def one(axis_at, blocks):
        draws = jax.random.uniform(jax.random.fold_in(jax.random.fold_in(own_key, 6), axis_at), (blocks,), jnp.float32, least / len(cuts), largest / len(cuts))
        return jnp.repeat(jnp.exp(draws), dims[axis_at] // blocks).reshape((-1,) + (1,) * (len(dims) - axis_at - 1))

    loudness = one(*cuts[0])
    for cut in cuts[1:]:
        loudness = loudness * one(*cut)
    return loudness


def shared_out(own_key, own, number, rows, count, top, bound, skew):
    sequence = jax.random.permutation(own_key, count)
    heavy_load, common = shares(count, rows * top, bound, skew, True), shares(count, rows * top, bound, skew, False)
    places = jnp.arange(count)

    def named(tallies, turn):
        used = int((tallies > 0).sum())
        fixed = max(1, used // 4)
        passed = fixed + (places - fixed + turn * (used - fixed)) % max(1, count - fixed)
        return jnp.zeros((count,), jnp.int32).at[sequence[jnp.where(places < fixed, places, passed)]].set(jnp.asarray(tallies, jnp.int32))

    tallies = jnp.where(number % 4 == 0, named(heavy_load, number // 4), named(common, number - number // 4 - 1))
    mixed = jax.random.permutation(jax.random.fold_in(own, 3), count)
    giver, sink = mixed[0:count // 2 * 2:2], mixed[1:count // 2 * 2:2]
    slack = jnp.minimum(tallies[giver] - 1, bound - tallies[sink]) // 2
    slack = jnp.where((giver == sequence[0]) | (sink == sequence[0]) | (tallies[sink] == 0), 0, jnp.maximum(slack, 0))
    passed = jax.random.randint(jax.random.fold_in(own, 4), (count // 2,), 0, 1 << 20) % (slack + 1)
    tallies = tallies.at[giver].add(-passed).at[sink].add(passed)
    labels = jnp.searchsorted(jnp.cumsum(tallies), jnp.arange(rows * top), side="right").astype(jnp.int32)
    listing = labels.reshape(top, rows).T
    listing = listing[jax.random.permutation(jax.random.fold_in(own, 1), rows)]
    turn = jax.random.randint(jax.random.fold_in(own, 2), (rows, 1), 0, top)
    return jnp.take_along_axis(listing, (jnp.arange(top)[None, :] + turn) % top, axis=1)


def shares(number_of, total, bound, skew, full):
    portions = [(1 << 20) // math.isqrt(rank ** skew) + 1 for rank in range(1, number_of + 1)]
    largest = bound if full else min(bound, max(-(-total // number_of), total * portions[0] // sum(portions)))
    least = 1 if total - largest >= number_of - 1 else 0
    holding, rest = [largest] + [least] * (number_of - 1), total - largest - least * (number_of - 1)
    while rest > 0:
        candidates = [i for i in range(1, number_of) if holding[i] < largest] or [i for i in range(1, number_of) if holding[i] < bound]
        pool, remaining = sum([portions[i] for i in candidates]), rest
        for i in candidates:
            extra = min(bound - holding[i], max(1, remaining * portions[i] // pool), rest)
            holding[i] = holding[i] + extra
            rest = rest - extra
    return np.array(holding)


def normal_values(rng, extent, scale, reach, cuts=(), kind=jnp.bfloat16):
    drawn = jax.random.normal(rng, extent, jnp.float32) * scale
    if len(cuts) > 0:
        drawn = level_of(rng, extent, cuts, -0.22, 0.18) * drawn
    return jnp.clip(drawn, min=-reach, max=reach).astype(kind)


def setup_inputs(seed: int = 0) -> dict:
    keys = jax.random.split(jax.random.key(seed), 7)
    panel = draw_panel(jax.random.fold_in(keys[6], 71), 0)
    trailing = normal_values(keys[1], (M, W), 1.0, 6.0, ((0, 8), (1, 16)), jnp.float32)
    factors = normal_values(keys[2], (ITEMS, TB, 2 * RK), 0.2, 1.1953125, ((0, 128),))
    owner_keys = jax.random.split(jax.random.fold_in(keys[3], 1), ITEMS // ITEMS_DEV)
    owner_turns = jax.random.permutation(jax.random.fold_in(keys[3], 3), ITEMS // ITEMS_DEV)
    owner = jax.vmap(lambda own, number: shared_out(jax.random.fold_in(keys[3], 2), own, number, ITEMS_DEV, DEVICES, 1, CAP, 2))(owner_keys, owner_turns).reshape((ITEMS, 1))
    tile_slot = plant(jax.random.randint(keys[4], (ITEMS,), 0, N_COL), jax.random.fold_in(keys[4], 1), 0, N_COL - 1).astype(jnp.int32)
    ranks = plant(jax.random.randint(keys[5], (ITEMS,), RK // 2, RK + 1), jax.random.fold_in(keys[5], 1), RK // 2, RK).astype(jnp.int32)
    return dict(panel=panel, trailing=trailing, factors=factors, owner=owner, tile_slot=tile_slot, ranks=ranks)


def reference(panel, trailing, factors, owner, tile_slot, ranks):
    factor = jnp.linalg.cholesky(panel[:TB])
    inverse = lax.linalg.triangular_solve(factor, jnp.eye(TB, dtype=panel.dtype), left_side=True, lower=True)
    lower = jnp.dot(panel, inverse.T, precision=lax.Precision.HIGHEST)
    columns = lower[TB * N_COL:TB * N_COL + W]
    update = jnp.dot(lower, columns.T, precision=lax.Precision.HIGHEST)
    dest = owner[:, 0]
    tile_row = dest // N_COL * N_COL + tile_slot
    tile_col = dest % N_COL
    col_index = jnp.arange(2 * RK)
    keep = (col_index[None, :] >= RK) | (col_index[None, :] < ranks[:, None])
    masked = jnp.where(keep[:, None, :], factors, jnp.zeros_like(factors))
    blocks = masked.reshape(DEVICES, ITEMS_DEV, TB, 2 * RK)
    rows_blocks = tile_row.reshape(DEVICES, ITEMS_DEV)
    cols_blocks = tile_col.reshape(DEVICES, ITEMS_DEV)

    def absorb(tiles, block):
        pieces, rows_here, cols_here = block
        pieces = pieces.astype(jnp.float32)
        dense = jnp.einsum('sak,sbk->sab', pieces[..., :RK], pieces[..., RK:], precision=lax.Precision.HIGHEST)
        return (tiles.at[rows_here, cols_here].add(dense), None)
    tiles = jnp.zeros((M // TB, N_COL, TB, TB), jnp.float32)
    tiles, _ = lax.scan(absorb, tiles, (blocks, rows_blocks, cols_blocks))
    extend = tiles.transpose(0, 2, 1, 3).reshape(M, W)
    updated = trailing + extend - update
    return (updated, lower)
```

```python
import jax
import jax.numpy as jnp
from jax import lax
from jax.experimental import pallas as pl
from jax.experimental.pallas import tpu as pltpu
from jax.sharding import PartitionSpec as P

ALL = ("row", "col")
HIGHEST = lax.Precision.HIGHEST
VMEM_LIMIT = 48 * 1024 * 1024


def pack(target, factors, devices):
    items, rows, width = factors.shape
    chunk = 16

    def kernel(target_ref, factors_ref, first_ref, second_ref, held, load_sems, store_sems):
        def load(c):
            part = pl.ds(c * chunk, chunk)
            return pltpu.make_async_copy(factors_ref.at[part], held.at[part], load_sems.at[c])

        @pl.loop(0, items // chunk)
        def _(c):
            load(c).start()

        @pl.loop(0, items // chunk)
        def _(c):
            load(c).wait()

            @pl.loop(0, chunk)
            def _(i):
                k = c * chunk + i
                place = target_ref[k]

                @pl.when(place < devices)
                def _():
                    pltpu.make_async_copy(held.at[k], first_ref.at[place], store_sems.at[k]).start()

                @pl.when(place >= devices)
                def _():
                    pltpu.make_async_copy(held.at[k], second_ref.at[place - devices], store_sems.at[k]).start()

        @pl.loop(0, items)
        def _(k):
            pltpu.make_async_copy(held.at[k], first_ref.at[0], store_sems.at[k]).wait()

    box = jax.ShapeDtypeStruct((devices, rows, width), factors.dtype)
    size = items * rows * width * 2
    return pl.pallas_call(
        kernel,
        out_shape=(box, box),
        grid_spec=pltpu.PrefetchScalarGridSpec(
            num_scalar_prefetch=1,
            grid=(1,),
            in_specs=[pl.BlockSpec(memory_space=pl.ANY)],
            out_specs=[pl.BlockSpec(memory_space=pl.ANY)] * 2,
            scratch_shapes=[
                pltpu.VMEM((items, rows, width), factors.dtype),
                pltpu.SemaphoreType.DMA((items // chunk,)),
                pltpu.SemaphoreType.DMA((items,)),
            ],
        ),
        compiler_params=pltpu.CompilerParams(vmem_limit_bytes=VMEM_LIMIT),
        cost_estimate=pl.CostEstimate(flops=0, bytes_accessed=2 * size, transcendentals=0),
        name="pack",
    )(target, factors)


def absorb(tags, inbox, base, tiles):
    slots, rows, width = inbox.shape
    half = width // 2
    chunk = 16

    def kernel(tags_ref, inbox_ref, base_ref, out_ref):
        step = pl.program_id(0)

        @pl.when(step == 0)
        def _():
            out_ref[...] = base_ref[...]

        lane = lax.broadcasted_iota(jnp.int32, (rows, half), 1)

        @pl.loop(0, chunk)
        def _(i):
            tag = tags_ref[step * chunk + i]

            @pl.when(tag >= 0)
            def _():
                slot = tag // 64
                rank = tag % 64 + 1
                left = jnp.where(lane < rank, inbox_ref[i, :, :half], jnp.bfloat16(0))
                right = inbox_ref[i, :, half:]
                out_ref[slot] += lax.dot_general(
                    left, right, (((1,), (1,)), ((), ())), preferred_element_type=jnp.float32
                )

    whole = pl.BlockSpec((tiles, rows, rows), lambda s, t: (0, 0, 0))
    return pl.pallas_call(
        kernel,
        out_shape=jax.ShapeDtypeStruct((tiles, rows, rows), jnp.float32),
        grid_spec=pltpu.PrefetchScalarGridSpec(
            num_scalar_prefetch=1,
            grid=(slots // chunk,),
            in_specs=[pl.BlockSpec((chunk, rows, width), lambda s, t: (s, 0, 0)), whole],
            out_specs=whole,
        ),
        compiler_params=pltpu.CompilerParams(vmem_limit_bytes=VMEM_LIMIT),
        cost_estimate=pl.CostEstimate(
            flops=2 * slots * rows * rows * half,
            bytes_accessed=slots * rows * width * 2 + 8 * tiles * rows * rows,
            transcendentals=0,
        ),
        name="absorb",
    )(tags, inbox, base)


def shards(panel, trailing, factors, owner, tile_slot, ranks):
    rows_devs = lax.axis_size("row")
    cols_devs = lax.axis_size("col")
    devices = rows_devs * cols_devs
    items = factors.shape[0]
    tile = panel.shape[0]
    me = lax.axis_index("row") * cols_devs + lax.axis_index("col")

    dest = owner[:, 0]
    order = jnp.arange(items)
    earlier = (dest[:, None] == dest[None, :]) & (order[:, None] > order[None, :])
    target = dest + devices * jnp.any(earlier, axis=1).astype(jnp.int32)
    first_out, second_out = pack(target, factors, devices)

    def spread(value, steps):
        for pairs in steps:
            value = value + sum([lax.ppermute(value, ALL, p) for p in pairs])
        return value

    along_x = [[(0, r * cols_devs)] for r in range(2, rows_devs, 2)]
    evens = [r * cols_devs for r in range(0, rows_devs, 2)]
    along_y = [[(e, e + y) for e in evens] for y in range(1, 4)]
    along_z = [[(e + y, e + y + z) for e in evens for y in range(4)] for z in range(4, cols_devs, 4)]
    across = [[(e + c, e + c + cols_devs) for e in evens for c in range(cols_devs)]]
    diagonal = spread(
        jnp.where(me == 0, panel, jnp.zeros_like(panel)), [along_x, along_y, along_z, across]
    )

    code = ((dest * 16 + tile_slot) * 64 + ranks - 1).astype(jnp.float32)
    label = jnp.zeros((8, tile), jnp.float32).at[0, :items].set(code)
    by_row = lax.all_gather(jnp.concatenate([panel, label]), "row", axis=0).reshape(rows_devs, tile + 8, tile)
    columns_panel = by_row[1, :tile]
    by_col = lax.all_gather(jnp.concatenate([panel, by_row[:, tile]]), "col", axis=0)
    front = by_col[:, :tile].reshape(cols_devs * tile, tile)
    codes = by_col[:, tile:, :items].transpose(1, 0, 2).reshape(devices, items).astype(jnp.int32)
    mine = codes // 1024 == me
    place = jnp.arange(items)[None, :]
    first = jnp.min(jnp.where(mine, place, items), axis=1)
    last = jnp.max(jnp.where(mine, place, -1), axis=1)
    first_tags = jnp.max(jnp.where(mine & (place == first[:, None]), codes % 1024, -1), axis=1)
    second_tags = jnp.max(
        jnp.where(mine & (place == last[:, None]) & (first < last)[:, None], codes % 1024, -1), axis=1
    )

    factor = jnp.linalg.cholesky(diagonal)
    inverse = lax.linalg.triangular_solve(
        factor, jnp.eye(tile, dtype=jnp.float32), left_side=True, lower=True
    )
    lower = jnp.dot(panel, inverse.T, precision=HIGHEST)
    columns = jnp.dot(columns_panel, inverse.T, precision=HIGHEST)
    weights = jnp.dot(inverse.T, columns.T, precision=HIGHEST)
    base = trailing - jnp.dot(front, weights, precision=HIGHEST)

    first_in = lax.all_to_all(first_out, ALL, split_axis=0, concat_axis=0, tiled=True)
    second_in = lax.all_to_all(second_out, ALL, split_axis=0, concat_axis=0, tiled=True)
    total = absorb(first_tags, first_in, base.reshape(cols_devs, tile, tile), cols_devs)
    total = absorb(second_tags, second_in, total, cols_devs)
    return (total.reshape(cols_devs * tile, tile), lower)


def solution(mesh):
    return jax.shard_map(
        shards,
        mesh=mesh,
        in_specs=(
            P(ALL, None),
            P("row", "col"),
            P(ALL, None, None),
            P(ALL, None),
            P(ALL),
            P(ALL),
        ),
        out_specs=(P("row", "col"), P(ALL, None)),
        check_vma=False,
    )
```

```python
import jax
import jax.numpy as jnp
from jax import lax
from jax.experimental import pallas as pl
from jax.experimental.pallas import tpu as pltpu
from jax.sharding import Mesh
from jax.sharding import PartitionSpec as P

ALL = ("x", "core", "z", "y")
ROW = ("x", "core")
COL = ("z", "y")
GROUP = 4
UNROLL = 4
SCHEDULED_FLOPS = 2 * 10**11
HIGHEST = lax.Precision.HIGHEST
PACK_VMEM = 58 * 1024 * 1024
ABSORB_VMEM = 58 * 1024 * 1024


def pack(target, labels, factors, devices):
    items, rows, width = factors.shape
    extra = labels.shape[1]
    chunk = 16

    def kernel(target_ref, labels_ref, factors_ref, first_ref, second_ref, held, load_sems, store_sems, label_sem):
        def load(c):
            part = pl.ds(c * chunk, chunk)
            return pltpu.make_async_copy(factors_ref.at[part], held.at[part], load_sems.at[c])

        def to_first(k, place):
            return pltpu.make_async_copy(held.at[k], first_ref.at[place, pl.ds(0, rows)], store_sems.at[k])

        def to_second(k, place):
            return pltpu.make_async_copy(held.at[k], second_ref.at[place], store_sems.at[k])

        @pl.loop(0, items // chunk)
        def _(c):
            load(c).start()

        tail = pltpu.make_async_copy(labels_ref, first_ref.at[:, pl.ds(rows, extra)], label_sem)
        tail.start()

        @pl.loop(0, items // chunk)
        def _(c):
            load(c).wait()

            @pl.loop(0, chunk)
            def _(i):
                k = c * chunk + i
                place = target_ref[k]

                @pl.when(place < devices)
                def _():
                    to_first(k, place).start()

                @pl.when(place >= devices)
                def _():
                    to_second(k, place - devices).start()

        tail.wait()

        @pl.loop(0, items)
        def _(k):
            to_second(k, 0).wait()

    size = items * rows * width * 2
    hbm = pl.BlockSpec(memory_space=pltpu.HBM)
    return pl.pallas_call(
        kernel,
        out_shape=(
            pltpu.HBM((devices, rows + extra, width), factors.dtype),
            pltpu.HBM((devices, rows, width), factors.dtype),
        ),
        in_specs=[pl.BlockSpec(memory_space=pltpu.SMEM), pl.BlockSpec(memory_space=pltpu.VMEM), hbm],
        out_specs=[hbm] * 2,
        scratch_shapes=[
            pltpu.VMEM((items, rows, width), factors.dtype),
            pltpu.SemaphoreType.DMA((items // chunk,)),
            pltpu.SemaphoreType.DMA((items,)),
            pltpu.SemaphoreType.DMA,
        ],
        compiler_params=pltpu.CompilerParams(vmem_limit_bytes=PACK_VMEM),
        cost_estimate=pl.CostEstimate(flops=0, bytes_accessed=2 * size, transcendentals=0),
        name="pack",
    )(target, labels, factors)


def plan(tags, tiles):
    slots = tags.shape[0]
    groups = slots // GROUP + tiles + UNROLL
    tile_of = jnp.where(tags >= 0, tags // 64, -1)
    order, tile = jnp.arange(slots), jnp.arange(tiles)
    before = jnp.sum((tile_of[:, None] == tile_of[None, :]) & (order[:, None] > order[None, :]), axis=1)
    need = (jnp.sum(tile_of[None, :] == tile[:, None], axis=1) + GROUP - 1) // GROUP
    end = jnp.sum(jnp.where(tile[None, :] <= tile[:, None], need[None, :], 0), axis=1)
    start = jnp.sum(jnp.where(tile_of[:, None] == tile[None, :], (end - need)[None, :], 0), axis=1)
    place = jnp.where(tags >= 0, start * GROUP + before, -1)
    entry = jnp.max(
        jnp.where(
            place[None, :] == jnp.arange(groups * GROUP)[:, None],
            (order * 128 + tags % 64 + 1)[None, :],
            -1,
        ),
        axis=1,
    )
    group_tile = jnp.sum((jnp.arange(groups)[:, None] >= end[None, :]).astype(jnp.int32), axis=1)
    return entry, jnp.minimum(group_tile, tiles - 1), end[tiles - 1 :]


def absorb(tags, inbox, base, update=()):
    slots, _, width = inbox.shape
    tiles, rows, _ = base.shape
    half = width // 2
    quarter = tiles // 4

    def kernel(entry_ref, tile_ref, count_ref, inbox_ref, base_ref, *refs):
        if update:
            front_ref, weights_ref, out_ref, held, total, sems, front = refs
        else:
            out_ref, held, total, sems = refs
        lane = lax.broadcasted_iota(jnp.int32, (16, width), 1)

        def load(q, kind):
            part = pl.ds(q * quarter, quarter)
            if kind:
                return pltpu.make_async_copy(front_ref.at[part], front.at[part], sems.at[4 + q])
            return pltpu.make_async_copy(base_ref.at[part], total.at[part], sems.at[q])

        for q in range(4):
            load(q, 0).start()
            if update:
                load(q, 1).start()
        items = pltpu.make_async_copy(inbox_ref.at[:, pl.ds(0, rows)], held, sems.at[8])
        items.start()

        for q in range(4):
            load(q, 0).wait()
            if update:
                load(q, 1).wait()

                @pl.loop(0, quarter // 2)
                def _(t):
                    pair = pl.ds(q * quarter + 2 * t, 2)
                    product = jnp.dot(
                        front[pair].reshape(2 * rows, rows),
                        weights_ref[...],
                        precision=HIGHEST,
                        preferred_element_type=jnp.float32,
                    )
                    total[pair] -= product.reshape(2, rows, rows)

        items.wait()

        def product(group):
            first = entry_ref[GROUP * group]
            first = jnp.where(first >= 0, first, entry_ref[0])

            def item(j):
                entry = entry_ref[GROUP * group + j]
                entry = jnp.where(entry >= 0, entry, (first // 128) * 128)
                return held[entry // 128], entry % 128

            left, right = [], []
            for j in range(0, GROUP, 2):
                (one, one_rank), (two, two_rank) = item(j), item(j + 1)
                keep = (lane < one_rank) | ((lane >= half) & (lane < half + two_rank))
                us = jnp.concatenate([one[:, :half], two[:, :half]], axis=1)
                us = us.reshape(rows // 16, 16, width) * keep.astype(us.dtype)[None]
                left.append(us.reshape(rows, width))
                right.append(jnp.concatenate([one[:, half:], two[:, half:]], axis=1))
            return lax.dot_general(
                jnp.concatenate(left, axis=1),
                jnp.concatenate(right, axis=1),
                (((1,), (1,)), ((), ())),
                preferred_element_type=jnp.float32,
            )

        @pl.loop(0, (count_ref[0] + UNROLL - 1) // UNROLL)
        def _(step):
            products = [product(step * UNROLL + u) for u in range(UNROLL)]
            for u in range(UNROLL):
                total[tile_ref[step * UNROLL + u]] += products[u]

        result = pltpu.make_async_copy(total, out_ref, sems.at[9])
        result.start()
        result.wait()

    smem, vmem = pl.BlockSpec(memory_space=pltpu.SMEM), pl.BlockSpec(memory_space=pltpu.VMEM)
    hbm = pl.BlockSpec(memory_space=pltpu.HBM)
    tiled = pltpu.VMEM(base.shape, base.dtype)
    return pl.pallas_call(
        kernel,
        out_shape=pltpu.HBM(base.shape, base.dtype),
        in_specs=[smem] * 3 + [hbm] * 2 + [hbm, vmem][: len(update)],
        out_specs=hbm,
        scratch_shapes=[pltpu.VMEM((slots, rows, width), inbox.dtype), tiled, pltpu.SemaphoreType.DMA((10,))]
        + [tiled][: len(update)],
        compiler_params=pltpu.CompilerParams(vmem_limit_bytes=ABSORB_VMEM),
        cost_estimate=pl.CostEstimate(
            flops=2 * slots * rows * rows * half,
            bytes_accessed=slots * rows * width * 2 + 8 * tiles * rows * rows,
            transcendentals=0,
        ),
        name="absorb",
    )(*plan(tags, tiles), inbox, base, *update)


def hold(array):
    def kernel(array_ref, out_ref):
        pass

    hbm = pl.BlockSpec(memory_space=pltpu.HBM)
    return pl.pallas_call(
        kernel,
        out_shape=pltpu.HBM(array.shape, array.dtype),
        in_specs=[hbm],
        out_specs=hbm,
        input_output_aliases={0: 0},
        cost_estimate=pl.CostEstimate(flops=SCHEDULED_FLOPS, bytes_accessed=0, transcendentals=0),
        name="hold",
    )(array)


def inverse_factor(block):
    half = block.shape[0] // 2
    eye = jnp.eye(half, dtype=block.dtype)

    def invert(part):
        factor = jnp.linalg.cholesky(part)
        return lax.linalg.triangular_solve(factor, eye, left_side=True, lower=True)

    first = invert(block[:half, :half])
    cross = 0.5 * (block[half:, :half] + block[:half, half:].T)
    below = jnp.dot(cross, first.T, precision=HIGHEST)
    second = invert(block[half:, half:] - jnp.dot(below, below.T, precision=HIGHEST))
    corner = -jnp.dot(second, jnp.dot(below, first, precision=HIGHEST), precision=HIGHEST)
    return jnp.concatenate(
        [jnp.concatenate([first, jnp.zeros_like(first)], axis=1), jnp.concatenate([corner, second], axis=1)]
    )


def shards(panel, trailing, factors, owner, tile_slot, ranks):
    rows_devs = lax.axis_size(ROW)
    cols_devs = lax.axis_size(COL)
    devices = rows_devs * cols_devs
    items = factors.shape[0]
    tile = panel.shape[0]
    me = lax.axis_index(ALL)

    dest = owner[:, 0]
    order = jnp.arange(items)
    same = dest[:, None] == dest[None, :]
    second = jnp.any(same & (order[:, None] > order[None, :]), axis=1)
    target = dest + devices * second.astype(jnp.int32)

    lands = target[None, :] == jnp.arange(2 * devices)[:, None]
    facts = jnp.stack([tile_slot, ranks])
    facts = jnp.max(jnp.where(lands[None], facts[:, None, :], 0), axis=2).reshape(2, 2, devices)
    facts = facts.transpose(2, 1, 0).reshape(devices, 1, 4).astype(factors.dtype)
    labels = jnp.pad(facts, ((0, 0), (0, 15), (0, factors.shape[2] - 4)))
    first_out, second_out = pack(target, labels, factors, devices)

    def spread(value, steps):
        return sum([lax.ppermute(value, ALL, pairs) for pairs in steps])

    def number(x, core, z, y):
        return ((x * 2 + core) * 4 + z) * 4 + y

    four = range(4)
    x, core = lax.axis_index("x"), lax.axis_index("core")

    front = lax.all_gather(panel, COL, axis=0, tiled=True)

    first_hop = [
        [(0, number(0, 0, 0, d))] + [(number(0, 1, z, y), number(d, 1, z, y)) for z in four for y in four]
        for d in (1, 2, 3)
    ]
    along_z = [[(number(0, 0, 0, y), number(0, 0, z, y)) for y in four] for z in (1, 2, 3)]
    along_x = [[(number(0, 0, z, y), number(x, 0, z, y)) for z in four for y in four] for x in (1, 2, 3)]
    swap = [[(number(x, c, z, y), number(x, 1 - c, z, y)) for x in four for c in (0, 1) for z in four for y in four]]
    held = jnp.where((me == 0) | ((x == 0) & (core == 1)), panel, spread(panel, first_hop))
    held, first_out, second_out = lax.optimization_barrier((held, first_out, second_out))
    for steps in (along_z, along_x):
        held = held + spread(held, steps)
    other = spread(held, swap)
    diagonal, columns_panel = jnp.where(core == 0, held, other), jnp.where(core == 0, other, held)

    diagonal, columns_panel, first_out = lax.optimization_barrier((diagonal, columns_panel, first_out))
    first_in = lax.all_to_all(first_out, ALL, split_axis=0, concat_axis=0, tiled=True)

    inverse = inverse_factor(diagonal)
    inverse, second_out = lax.optimization_barrier((inverse, second_out))
    second_in = lax.all_to_all(second_out, ALL, split_axis=0, concat_axis=0, tiled=True)

    facts = first_in[:, tile, :4].astype(jnp.int32)
    first_tags, second_tags = [facts[:, 2 * i] * 64 + facts[:, 2 * i + 1] - 1 for i in (0, 1)]

    lower = jnp.dot(panel, inverse.T, precision=HIGHEST)
    columns = jnp.dot(columns_panel, inverse.T, precision=HIGHEST)
    weights = jnp.dot(inverse.T, columns.T, precision=HIGHEST)
    tiled = (cols_devs, tile, tile)
    total = absorb(first_tags, first_in, trailing.reshape(tiled))
    front, total = lax.optimization_barrier((front.reshape(tiled), total))
    total = absorb(second_tags, second_in, total, (hold(front), weights))
    return (total.reshape(cols_devs * tile, tile), lower)


def solution(mesh):
    fine = Mesh(mesh.devices.reshape(4, 2, 4, 4), ALL)
    return jax.shard_map(
        shards,
        mesh=fine,
        in_specs=(
            P(ALL, None),
            P(ROW, COL),
            P(ALL, None, None),
            P(ALL, None),
            P(ALL),
            P(ALL),
        ),
        out_specs=(P(ROW, COL), P(ALL, None)),
        check_vma=False,
    )
```

```python
import jax
import jax.numpy as jnp
from jax import lax
from jax.experimental import pallas as pl
from jax.experimental.pallas import tpu as pltpu
from jax.sharding import Mesh
from jax.sharding import PartitionSpec as P

ALL = ("x", "core", "z", "y")
ROW = ("x", "core")
COL = ("z", "y")
GROUP = 4
UNROLL = 4
SCHEDULED_FLOPS = 2 * 10**11
HIGHEST = lax.Precision.HIGHEST
PACK_VMEM = 58 * 1024 * 1024
ABSORB_VMEM = 58 * 1024 * 1024


def pack(target, factors, devices, begin, end, boxes=(), labels=None):
    rows, width = factors.shape[1:]
    items, chunk, extra = end - begin, 16, 16
    labelled = [] if labels is None else [labels]

    def kernel(target_ref, factors_ref, *refs):
        first_ref, second_ref, held, load_sems, store_sems, label_sem = refs[-6:]

        def load(c):
            part = factors_ref.at[pl.ds(begin + c * chunk, chunk)]
            return pltpu.make_async_copy(part, held.at[pl.ds(c * chunk, chunk)], load_sems.at[c])

        def to_first(k, place):
            return pltpu.make_async_copy(held.at[k], first_ref.at[place, pl.ds(0, rows)], store_sems.at[k])

        def to_second(k, place):
            return pltpu.make_async_copy(held.at[k], second_ref.at[place], store_sems.at[k])

        @pl.loop(0, items // chunk)
        def _(c):
            load(c).start()

        if labelled:
            tail = pltpu.make_async_copy(refs[0], first_ref.at[:, pl.ds(rows, extra)], label_sem)
            tail.start()

        @pl.loop(0, items // chunk)
        def _(c):
            load(c).wait()

            @pl.loop(0, chunk)
            def _(i):
                k = c * chunk + i
                place = target_ref[begin + k]

                @pl.when(place < devices)
                def _():
                    to_first(k, place).start()

                @pl.when(place >= devices)
                def _():
                    to_second(k, place - devices).start()

        if labelled:
            tail.wait()

        @pl.loop(0, items)
        def _(k):
            to_second(k, 0).wait()

    hbm = pl.BlockSpec(memory_space=pltpu.HBM)
    before = 2 + len(labelled)
    return pl.pallas_call(
        kernel,
        out_shape=(
            pltpu.HBM((devices, rows + extra, width), factors.dtype),
            pltpu.HBM((devices, rows, width), factors.dtype),
        ),
        in_specs=[pl.BlockSpec(memory_space=pltpu.SMEM), hbm]
        + [pl.BlockSpec(memory_space=pltpu.VMEM)] * len(labelled)
        + [hbm] * len(boxes),
        out_specs=[hbm] * 2,
        input_output_aliases={before + i: i for i in range(len(boxes))},
        scratch_shapes=[
            pltpu.VMEM((items, rows, width), factors.dtype),
            pltpu.SemaphoreType.DMA((items // chunk,)),
            pltpu.SemaphoreType.DMA((items,)),
            pltpu.SemaphoreType.DMA,
        ],
        compiler_params=pltpu.CompilerParams(vmem_limit_bytes=PACK_VMEM),
        cost_estimate=pl.CostEstimate(flops=0, bytes_accessed=items * rows * width * 4, transcendentals=0),
        name="pack",
    )(target, factors, *labelled, *boxes)


def plan(tags, tiles):
    slots = tags.shape[0]
    groups = slots // GROUP + tiles + UNROLL
    tile_of = jnp.where(tags >= 0, tags // 64, -1)
    order, tile = jnp.arange(slots), jnp.arange(tiles)
    before = jnp.sum((tile_of[:, None] == tile_of[None, :]) & (order[:, None] > order[None, :]), axis=1)
    need = (jnp.sum(tile_of[None, :] == tile[:, None], axis=1) + GROUP - 1) // GROUP
    end = jnp.sum(jnp.where(tile[None, :] <= tile[:, None], need[None, :], 0), axis=1)
    start = jnp.sum(jnp.where(tile_of[:, None] == tile[None, :], (end - need)[None, :], 0), axis=1)
    place = jnp.where(tags >= 0, start * GROUP + before, -1)
    entry = jnp.max(
        jnp.where(
            place[None, :] == jnp.arange(groups * GROUP)[:, None],
            (order * 128 + tags % 64 + 1)[None, :],
            -1,
        ),
        axis=1,
    )
    group_tile = jnp.sum((jnp.arange(groups)[:, None] >= end[None, :]).astype(jnp.int32), axis=1)
    return entry, jnp.minimum(group_tile, tiles - 1), end[tiles - 1 :]


def absorb(tags, inbox, base):
    slots, _, width = inbox.shape
    tiles, rows, _ = base.shape
    half = width // 2

    def kernel(entry_ref, tile_ref, count_ref, inbox_ref, base_ref, out_ref, held, total, sems):
        lane = lax.broadcasted_iota(jnp.int32, (16, width), 1)
        copies = [
            pltpu.make_async_copy(inbox_ref.at[:, pl.ds(0, rows)], held, sems.at[0]),
            pltpu.make_async_copy(base_ref, total, sems.at[1]),
        ]
        for copy in copies:
            copy.start()
        for copy in copies:
            copy.wait()

        def product(group):
            first = entry_ref[GROUP * group]
            first = jnp.where(first >= 0, first, entry_ref[0])

            def item(j):
                entry = entry_ref[GROUP * group + j]
                entry = jnp.where(entry >= 0, entry, (first // 128) * 128)
                return held[entry // 128], entry % 128

            left, right = [], []
            for j in range(0, GROUP, 2):
                (one, one_rank), (two, two_rank) = item(j), item(j + 1)
                keep = (lane < one_rank) | ((lane >= half) & (lane < half + two_rank))
                us = jnp.concatenate([one[:, :half], two[:, :half]], axis=1)
                us = us.reshape(rows // 16, 16, width) * keep.astype(us.dtype)[None]
                left.append(us.reshape(rows, width))
                right.append(jnp.concatenate([one[:, half:], two[:, half:]], axis=1))
            return lax.dot_general(
                jnp.concatenate(left, axis=1),
                jnp.concatenate(right, axis=1),
                (((1,), (1,)), ((), ())),
                preferred_element_type=jnp.float32,
            )

        @pl.loop(0, (count_ref[0] + UNROLL - 1) // UNROLL)
        def _(step):
            products = [product(step * UNROLL + u) for u in range(UNROLL)]
            for u in range(UNROLL):
                total[tile_ref[step * UNROLL + u]] += products[u]

        result = pltpu.make_async_copy(total, out_ref, sems.at[2])
        result.start()
        result.wait()

    smem = pl.BlockSpec(memory_space=pltpu.SMEM)
    hbm = pl.BlockSpec(memory_space=pltpu.HBM)
    return pl.pallas_call(
        kernel,
        out_shape=pltpu.HBM(base.shape, base.dtype),
        in_specs=[smem] * 3 + [hbm] * 2,
        out_specs=hbm,
        scratch_shapes=[
            pltpu.VMEM((slots, rows, width), inbox.dtype),
            pltpu.VMEM(base.shape, base.dtype),
            pltpu.SemaphoreType.DMA((3,)),
        ],
        compiler_params=pltpu.CompilerParams(vmem_limit_bytes=ABSORB_VMEM),
        cost_estimate=pl.CostEstimate(
            flops=2 * slots * rows * rows * half,
            bytes_accessed=slots * rows * width * 2 + 8 * tiles * rows * rows,
            transcendentals=0,
        ),
        name="absorb",
    )(*plan(tags, tiles), inbox, base)


def subtract(base, front, weights):
    tiles, rows, depth = front.shape
    parts = 8
    size = tiles // parts

    def kernel(base_ref, front_ref, weights_ref, out_ref, total, held, sems):
        def copy(q, kind):
            part = pl.ds(q * size, size)
            ends = [(base_ref, total), (front_ref, held), (total, out_ref)][kind]
            return pltpu.make_async_copy(ends[0].at[part], ends[1].at[part], sems.at[kind, q])

        @pl.loop(0, parts)
        def _(q):
            copy(q, 0).start()
            copy(q, 1).start()

        @pl.loop(0, parts)
        def _(q):
            copy(q, 0).wait()
            copy(q, 1).wait()
            part = pl.ds(q * size, size)
            product = jnp.dot(
                held[part].reshape(size * rows, depth),
                weights_ref[...],
                precision=HIGHEST,
                preferred_element_type=jnp.float32,
            )
            total[part] -= product.reshape(size, rows, -1)
            copy(q, 2).start()

        @pl.loop(0, parts)
        def _(q):
            copy(q, 2).wait()

    hbm = pl.BlockSpec(memory_space=pltpu.HBM)
    return pl.pallas_call(
        kernel,
        out_shape=pltpu.HBM(base.shape, base.dtype),
        in_specs=[hbm, hbm, pl.BlockSpec(memory_space=pltpu.VMEM)],
        out_specs=hbm,
        scratch_shapes=[
            pltpu.VMEM(base.shape, base.dtype),
            pltpu.VMEM(front.shape, front.dtype),
            pltpu.SemaphoreType.DMA((3, parts)),
        ],
        compiler_params=pltpu.CompilerParams(vmem_limit_bytes=ABSORB_VMEM),
        cost_estimate=pl.CostEstimate(flops=SCHEDULED_FLOPS, bytes_accessed=3 * base.size * 4, transcendentals=0),
        name="subtract",
    )(base, front, weights)


def inverse_factor(block):
    half = block.shape[0] // 2
    eye = jnp.eye(half, dtype=block.dtype)

    def invert(part):
        factor = jnp.linalg.cholesky(part)
        return lax.linalg.triangular_solve(factor, eye, left_side=True, lower=True)

    first = invert(block[:half, :half])
    cross = 0.5 * (block[half:, :half] + block[:half, half:].T)
    below = jnp.dot(cross, first.T, precision=HIGHEST)
    second = invert(block[half:, half:] - jnp.dot(below, below.T, precision=HIGHEST))
    corner = -jnp.dot(second, jnp.dot(below, first, precision=HIGHEST), precision=HIGHEST)
    return jnp.concatenate(
        [jnp.concatenate([first, jnp.zeros_like(first)], axis=1), jnp.concatenate([corner, second], axis=1)]
    )


def shards(panel, trailing, factors, owner, tile_slot, ranks):
    rows_devs = lax.axis_size(ROW)
    cols_devs = lax.axis_size(COL)
    devices = rows_devs * cols_devs
    items = factors.shape[0]
    tile = panel.shape[0]
    me = lax.axis_index(ALL)

    dest = owner[:, 0]
    order = jnp.arange(items)
    same = dest[:, None] == dest[None, :]
    second = jnp.any(same & (order[:, None] > order[None, :]), axis=1)
    target = dest + devices * second.astype(jnp.int32)

    lands = target[None, :] == jnp.arange(2 * devices)[:, None]
    facts = jnp.stack([tile_slot, ranks])
    facts = jnp.max(jnp.where(lands[None], facts[:, None, :], 0), axis=2).reshape(2, 2, devices)
    facts = facts.transpose(2, 1, 0).reshape(devices, 1, 4).astype(factors.dtype)
    labels = jnp.pad(facts, ((0, 0), (0, 15), (0, factors.shape[2] - 4)))
    boxes = pack(target, factors, devices, 0, items // 2)

    def spread(value, steps):
        return sum([lax.ppermute(value, ALL, pairs) for pairs in steps])

    def number(x, core, z, y):
        return ((x * 2 + core) * 4 + z) * 4 + y

    four = range(4)
    x, core = lax.axis_index("x"), lax.axis_index("core")

    front = lax.all_gather(panel, COL, axis=0, tiled=True)

    first_hop = [
        [(0, number(0, 0, 0, d))] + [(number(0, 1, z, y), number(d, 1, z, y)) for z in four for y in four]
        for d in (1, 2, 3)
    ]
    along_z = [[(number(0, 0, 0, y), number(0, 0, z, y)) for y in four] for z in (1, 2, 3)]
    along_x = [[(number(0, 0, z, y), number(x, 0, z, y)) for z in four for y in four] for x in (1, 2, 3)]
    swap = [[(number(x, c, z, y), number(x, 1 - c, z, y)) for x in four for c in (0, 1) for z in four for y in four]]
    held = jnp.where((me == 0) | ((x == 0) & (core == 1)), panel, spread(panel, first_hop))
    held, boxes = lax.optimization_barrier((held, boxes))
    held = held + spread(held, along_z)
    boxes = pack(target, factors, devices, items // 2, items, boxes, labels)
    held, (first_out, second_out) = lax.optimization_barrier((held, boxes))
    held = held + spread(held, along_x)
    other = spread(held, swap)
    diagonal, columns_panel = jnp.where(core == 0, held, other), jnp.where(core == 0, other, held)

    diagonal, columns_panel, first_out = lax.optimization_barrier((diagonal, columns_panel, first_out))
    first_in = lax.all_to_all(first_out, ALL, split_axis=0, concat_axis=0, tiled=True)

    inverse = inverse_factor(diagonal)
    inverse, second_out = lax.optimization_barrier((inverse, second_out))
    second_in = lax.all_to_all(second_out, ALL, split_axis=0, concat_axis=0, tiled=True)

    facts = first_in[:, tile, :4].astype(jnp.int32)
    first_tags, second_tags = [facts[:, 2 * i] * 64 + facts[:, 2 * i + 1] - 1 for i in (0, 1)]

    lower = jnp.dot(panel, inverse.T, precision=HIGHEST)
    columns = jnp.dot(columns_panel, inverse.T, precision=HIGHEST)
    weights = jnp.dot(inverse.T, columns.T, precision=HIGHEST)
    tiled = (cols_devs, tile, tile)
    total = absorb(first_tags, first_in, trailing.reshape(tiled))
    total = subtract(total, front.reshape(tiled), weights)
    total = absorb(second_tags, second_in, total)
    return (total.reshape(cols_devs * tile, tile), lower)


def solution(mesh):
    fine = Mesh(mesh.devices.reshape(4, 2, 4, 4), ALL)
    return jax.shard_map(
        shards,
        mesh=fine,
        in_specs=(
            P(ALL, None),
            P(ROW, COL),
            P(ALL, None, None),
            P(ALL, None),
            P(ALL),
            P(ALL),
        ),
        out_specs=(P(ROW, COL), P(ALL, None)),
        check_vma=False,
    )
```

```python
import jax
import jax.numpy as jnp
from jax import lax
from jax.experimental import pallas as pl
from jax.experimental.pallas import tpu as pltpu
from jax.sharding import Mesh
from jax.sharding import PartitionSpec as P

ALL = ("x", "core", "z", "y")
ROW = ("x", "core")
COL = ("z", "y")
GROUP = 4
UNROLL = 4
PARTS = 8
SCHEDULED_FLOPS = 2 * 10**11
HIGHEST = lax.Precision.HIGHEST
PACK_VMEM = 58 * 1024 * 1024
ABSORB_VMEM = 58 * 1024 * 1024


def pack(target, factors, devices, begin, end, boxes=(), labels=None):
    rows, width = factors.shape[1:]
    items, chunk, extra = end - begin, 16, 16
    labelled = [] if labels is None else [labels]

    def kernel(target_ref, factors_ref, *refs):
        first_ref, second_ref, held, load_sems, store_sems, label_sem = refs[-6:]

        def load(c):
            part = factors_ref.at[pl.ds(begin + c * chunk, chunk)]
            return pltpu.make_async_copy(part, held.at[pl.ds(c * chunk, chunk)], load_sems.at[c])

        def to_first(k, place):
            return pltpu.make_async_copy(held.at[k], first_ref.at[place, pl.ds(0, rows)], store_sems.at[k])

        def to_second(k, place):
            return pltpu.make_async_copy(held.at[k], second_ref.at[place], store_sems.at[k])

        @pl.loop(0, items // chunk)
        def _(c):
            load(c).start()

        if labelled:
            tail = pltpu.make_async_copy(refs[0], first_ref.at[:, pl.ds(rows, extra)], label_sem)
            tail.start()

        @pl.loop(0, items // chunk)
        def _(c):
            load(c).wait()

            @pl.loop(0, chunk)
            def _(i):
                k = c * chunk + i
                place = target_ref[begin + k]

                @pl.when(place < devices)
                def _():
                    to_first(k, place).start()

                @pl.when(place >= devices)
                def _():
                    to_second(k, place - devices).start()

        if labelled:
            tail.wait()

        @pl.loop(0, items)
        def _(k):
            to_second(k, 0).wait()

    hbm = pl.BlockSpec(memory_space=pltpu.HBM)
    before = 2 + len(labelled)
    return pl.pallas_call(
        kernel,
        out_shape=(
            pltpu.HBM((devices, rows + extra, width), factors.dtype),
            pltpu.HBM((devices, rows, width), factors.dtype),
        ),
        in_specs=[pl.BlockSpec(memory_space=pltpu.SMEM), hbm]
        + [pl.BlockSpec(memory_space=pltpu.VMEM)] * len(labelled)
        + [hbm] * len(boxes),
        out_specs=[hbm] * 2,
        input_output_aliases={before + i: i for i in range(len(boxes))},
        scratch_shapes=[
            pltpu.VMEM((items, rows, width), factors.dtype),
            pltpu.SemaphoreType.DMA((items // chunk,)),
            pltpu.SemaphoreType.DMA((items,)),
            pltpu.SemaphoreType.DMA,
        ],
        compiler_params=pltpu.CompilerParams(vmem_limit_bytes=PACK_VMEM),
        cost_estimate=pl.CostEstimate(flops=0, bytes_accessed=items * rows * width * 4, transcendentals=0),
        name="pack",
    )(target, factors, *labelled, *boxes)


def plan(tags, tiles):
    slots = tags.shape[0]
    groups = slots // GROUP + tiles + UNROLL
    tile_of = jnp.where(tags >= 0, tags // 64, -1)
    order, tile = jnp.arange(slots), jnp.arange(tiles)
    before = jnp.sum((tile_of[:, None] == tile_of[None, :]) & (order[:, None] > order[None, :]), axis=1)
    need = (jnp.sum(tile_of[None, :] == tile[:, None], axis=1) + GROUP - 1) // GROUP
    end = jnp.sum(jnp.where(tile[None, :] <= tile[:, None], need[None, :], 0), axis=1)
    start = jnp.sum(jnp.where(tile_of[:, None] == tile[None, :], (end - need)[None, :], 0), axis=1)
    place = jnp.where(tags >= 0, start * GROUP + before, -1)
    entry = jnp.max(
        jnp.where(
            place[None, :] == jnp.arange(groups * GROUP)[:, None],
            (order * 128 + tags % 64 + 1)[None, :],
            -1,
        ),
        axis=1,
    )
    group_tile = jnp.sum((jnp.arange(groups)[:, None] >= end[None, :]).astype(jnp.int32), axis=1)
    return entry, jnp.minimum(group_tile, tiles - 1), end[tiles - 1 :]


def absorb(tags, inbox, base):
    slots, _, width = inbox.shape
    tiles, rows, _ = base.shape
    half = width // 2

    def kernel(entry_ref, tile_ref, count_ref, inbox_ref, base_ref, out_ref, held, total, sems):
        lane = lax.broadcasted_iota(jnp.int32, (16, width), 1)
        def load(c):
            part = pl.ds(c * (slots // PARTS), slots // PARTS)
            return pltpu.make_async_copy(inbox_ref.at[part, pl.ds(0, rows)], held.at[part], sems.at[0, c])

        def sums(c, kind):
            part = pl.ds(c * (tiles // PARTS), tiles // PARTS)
            ends = (total, out_ref) if kind else (base_ref, total)
            return pltpu.make_async_copy(ends[0].at[part], ends[1].at[part], sems.at[1 + kind, c])

        @pl.loop(0, PARTS)
        def _(c):
            load(c).start()
            sums(c, 0).start()

        @pl.loop(0, PARTS)
        def _(c):
            load(c).wait()
            sums(c, 0).wait()

        def product(group):
            first = entry_ref[GROUP * group]
            first = jnp.where(first >= 0, first, entry_ref[0])

            def item(j):
                entry = entry_ref[GROUP * group + j]
                entry = jnp.where(entry >= 0, entry, (first // 128) * 128)
                return held[entry // 128], entry % 128

            left, right = [], []
            for j in range(0, GROUP, 2):
                (one, one_rank), (two, two_rank) = item(j), item(j + 1)
                keep = (lane < one_rank) | ((lane >= half) & (lane < half + two_rank))
                us = jnp.concatenate([one[:, :half], two[:, :half]], axis=1)
                us = us.reshape(rows // 16, 16, width) * keep.astype(us.dtype)[None]
                left.append(us.reshape(rows, width))
                right.append(jnp.concatenate([one[:, half:], two[:, half:]], axis=1))
            return lax.dot_general(
                jnp.concatenate(left, axis=1),
                jnp.concatenate(right, axis=1),
                (((1,), (1,)), ((), ())),
                preferred_element_type=jnp.float32,
            )

        @pl.loop(0, (count_ref[0] + UNROLL - 1) // UNROLL)
        def _(step):
            products = [product(step * UNROLL + u) for u in range(UNROLL)]
            for u in range(UNROLL):
                total[tile_ref[step * UNROLL + u]] += products[u]

        @pl.loop(0, PARTS)
        def _(c):
            sums(c, 1).start()

        @pl.loop(0, PARTS)
        def _(c):
            sums(c, 1).wait()

    smem = pl.BlockSpec(memory_space=pltpu.SMEM)
    hbm = pl.BlockSpec(memory_space=pltpu.HBM)
    return pl.pallas_call(
        kernel,
        out_shape=pltpu.HBM(base.shape, base.dtype),
        in_specs=[smem] * 3 + [hbm] * 2,
        out_specs=hbm,
        scratch_shapes=[
            pltpu.VMEM((slots, rows, width), inbox.dtype),
            pltpu.VMEM(base.shape, base.dtype),
            pltpu.SemaphoreType.DMA((3, PARTS)),
        ],
        compiler_params=pltpu.CompilerParams(vmem_limit_bytes=ABSORB_VMEM),
        cost_estimate=pl.CostEstimate(
            flops=2 * slots * rows * rows * half,
            bytes_accessed=slots * rows * width * 2 + 8 * tiles * rows * rows,
            transcendentals=0,
        ),
        name="absorb",
    )(*plan(tags, tiles), inbox, base)


def subtract(base, front, weights):
    tiles, rows, depth = front.shape
    parts = 8
    size = tiles // parts

    def kernel(base_ref, front_ref, weights_ref, out_ref, total, held, sems):
        def copy(q, kind):
            part = pl.ds(q * size, size)
            ends = [(base_ref, total), (front_ref, held), (total, out_ref)][kind]
            return pltpu.make_async_copy(ends[0].at[part], ends[1].at[part], sems.at[kind, q])

        @pl.loop(0, parts)
        def _(q):
            copy(q, 0).start()
            copy(q, 1).start()

        @pl.loop(0, parts)
        def _(q):
            copy(q, 0).wait()
            copy(q, 1).wait()
            part = pl.ds(q * size, size)
            product = jnp.dot(
                held[part].reshape(size * rows, depth),
                weights_ref[...],
                precision=HIGHEST,
                preferred_element_type=jnp.float32,
            )
            total[part] -= product.reshape(size, rows, -1)
            copy(q, 2).start()

        @pl.loop(0, parts)
        def _(q):
            copy(q, 2).wait()

    hbm = pl.BlockSpec(memory_space=pltpu.HBM)
    return pl.pallas_call(
        kernel,
        out_shape=pltpu.HBM(base.shape, base.dtype),
        in_specs=[hbm, hbm, pl.BlockSpec(memory_space=pltpu.VMEM)],
        out_specs=hbm,
        scratch_shapes=[
            pltpu.VMEM(base.shape, base.dtype),
            pltpu.VMEM(front.shape, front.dtype),
            pltpu.SemaphoreType.DMA((3, parts)),
        ],
        compiler_params=pltpu.CompilerParams(vmem_limit_bytes=ABSORB_VMEM),
        cost_estimate=pl.CostEstimate(flops=SCHEDULED_FLOPS, bytes_accessed=3 * base.size * 4, transcendentals=0),
        name="subtract",
    )(base, front, weights)


def inverse_factor(block):
    half = block.shape[0] // 2
    eye = jnp.eye(half, dtype=block.dtype)

    def invert(part):
        factor = jnp.linalg.cholesky(part)
        return lax.linalg.triangular_solve(factor, eye, left_side=True, lower=True)

    first = invert(block[:half, :half])
    cross = 0.5 * (block[half:, :half] + block[:half, half:].T)
    below = jnp.dot(cross, first.T, precision=HIGHEST)
    second = invert(block[half:, half:] - jnp.dot(below, below.T, precision=HIGHEST))
    corner = -jnp.dot(second, jnp.dot(below, first, precision=HIGHEST), precision=HIGHEST)
    return jnp.concatenate(
        [jnp.concatenate([first, jnp.zeros_like(first)], axis=1), jnp.concatenate([corner, second], axis=1)]
    )


def shards(panel, trailing, factors, owner, tile_slot, ranks):
    rows_devs = lax.axis_size(ROW)
    cols_devs = lax.axis_size(COL)
    devices = rows_devs * cols_devs
    items = factors.shape[0]
    tile = panel.shape[0]
    me = lax.axis_index(ALL)

    dest = owner[:, 0]
    order = jnp.arange(items)
    same = dest[:, None] == dest[None, :]
    second = jnp.any(same & (order[:, None] > order[None, :]), axis=1)
    target = dest + devices * second.astype(jnp.int32)

    lands = target[None, :] == jnp.arange(2 * devices)[:, None]
    facts = jnp.stack([tile_slot, ranks])
    facts = jnp.max(jnp.where(lands[None], facts[:, None, :], 0), axis=2).reshape(2, 2, devices)
    facts = facts.transpose(2, 1, 0).reshape(devices, 1, 4).astype(factors.dtype)
    labels = jnp.pad(facts, ((0, 0), (0, 15), (0, factors.shape[2] - 4)))
    boxes = pack(target, factors, devices, 0, items // 2)

    def spread(value, steps):
        return sum([lax.ppermute(value, ALL, pairs) for pairs in steps])

    def number(x, core, z, y):
        return ((x * 2 + core) * 4 + z) * 4 + y

    four = range(4)
    x, core = lax.axis_index("x"), lax.axis_index("core")

    front = lax.all_gather(panel, COL, axis=0, tiled=True)

    first_hop = [
        [(0, number(0, 0, 0, d))] + [(number(0, 1, z, y), number(d, 1, z, y)) for z in four for y in four]
        for d in (1, 2, 3)
    ]
    along_z = [[(number(0, 0, 0, y), number(0, 0, z, y)) for y in four] for z in (1, 2, 3)]
    along_x = [[(number(0, 0, z, y), number(x, 0, z, y)) for z in four for y in four] for x in (1, 2, 3)]
    swap = [[(number(x, c, z, y), number(x, 1 - c, z, y)) for x in four for c in (0, 1) for z in four for y in four]]
    held = jnp.where((me == 0) | ((x == 0) & (core == 1)), panel, spread(panel, first_hop))
    held, boxes = lax.optimization_barrier((held, boxes))
    held = held + spread(held, along_z)
    boxes = pack(target, factors, devices, items // 2, items, boxes, labels)
    held, (first_out, second_out) = lax.optimization_barrier((held, boxes))
    held = held + spread(held, along_x)
    other = spread(held, swap)
    diagonal, columns_panel = jnp.where(core == 0, held, other), jnp.where(core == 0, other, held)

    diagonal, columns_panel, first_out = lax.optimization_barrier((diagonal, columns_panel, first_out))
    first_in = lax.all_to_all(first_out, ALL, split_axis=0, concat_axis=0, tiled=True)

    inverse = inverse_factor(diagonal)
    inverse, second_out = lax.optimization_barrier((inverse, second_out))
    second_in = lax.all_to_all(second_out, ALL, split_axis=0, concat_axis=0, tiled=True)

    facts = first_in[:, tile, :4].astype(jnp.int32)
    first_tags, second_tags = [facts[:, 2 * i] * 64 + facts[:, 2 * i + 1] - 1 for i in (0, 1)]

    lower = jnp.dot(panel, inverse.T, precision=HIGHEST)
    columns = jnp.dot(columns_panel, inverse.T, precision=HIGHEST)
    weights = jnp.dot(inverse.T, columns.T, precision=HIGHEST)
    tiled = (cols_devs, tile, tile)
    total = absorb(first_tags, first_in, trailing.reshape(tiled))
    total = subtract(total, front.reshape(tiled), weights)
    total = absorb(second_tags, second_in, total)
    return (total.reshape(cols_devs * tile, tile), lower)


def solution(mesh):
    fine = Mesh(mesh.devices.reshape(4, 2, 4, 4), ALL)
    return jax.shard_map(
        shards,
        mesh=fine,
        in_specs=(
            P(ALL, None),
            P(ROW, COL),
            P(ALL, None, None),
            P(ALL, None),
            P(ALL),
            P(ALL),
        ),
        out_specs=(P(ROW, COL), P(ALL, None)),
        check_vma=False,
    )
```
